32 devices in a mesh: seq: 8 (over z, x), kvh: 4 (over y, core).
Axes of the slice: x: 2, y: 2, z: 4, core: 2. Of those that a mesh axis runs over, the one named last changes fastest.
Arguments:
- queries: bfloat16 [4096, 5120], P(('seq', 'kvh')), may hold values from -32 to 32, as said below
- keys: bfloat16 [4096, 1024], P(('seq', 'kvh')), may hold values from -6 to 6, as said below
- doc_ids: int32 [4096], P('seq'), may hold values from 0 to 1, never falling along the last dimension, each value on 1 to 3585 neighbouring positions
Outputs:
- col_scores: float32 [40, 4096], P('kvh', 'seq')
The draws below stay inside these ranges and needn't reach their ends.
Inputs may be any that keep to these rules, and one draw needn't show every extreme that they name: `doc_ids`: document numbers never fall along the window; every document has 1 to 3585 tokens. `queries`: finite values. `keys`: finite values.
All inputs are finite; a program needn't handle non-finite values.
Results may differ from the reference program's by a relative error of at most 0.0003.
Values may be sent and summed in bfloat16 or wider, within the bound.
A program may use at most 320 MiB of HBM per device.

```python
import math
import jax
import jax.numpy as jnp
import numpy as np
from jax import lax

QH = 40
KVH = 8
HD = 128
TOK_DEV = 512
REACH_DEV = 8
TOKENS = 4096
DOCS = 2
DOC_MOST = 3585


def joint_fields(key):
    base = jax.random.fold_in(key, 11)
    key_q, key_k = jax.random.split(base, 2)
    query_field = jnp.clip(jax.random.normal(key_q, (TOKENS, QH, HD), jnp.float32), -5.5, 5.5)
    key_field = jnp.clip(jax.random.normal(key_k, (TOKENS, KVH, HD), jnp.float32), -5.5, 5.5)
    return (query_field, key_field)


def draw_queries(key, part):
    return joint_fields(key)[0].reshape(TOKENS, QH * HD).astype(jnp.bfloat16)


def draw_keys(key, part):
    return joint_fields(key)[1].reshape(TOKENS, KVH * HD).astype(jnp.bfloat16)


def length_profile(number_of, total, most, slope):
    portions = [(1 << 20) // math.isqrt(grade ** slope) + 1 for grade in range(2, number_of + 1)]
    spare, holding = total - most - (number_of - 1), [1] * (number_of - 1)
    while spare > 0:
        movable = [i for i in range(number_of - 1) if holding[i] < most]
        whole, left = sum([portions[i] for i in movable]), spare
        for i in movable:
            more = min(most - holding[i], max(1, left * portions[i] // whole), spare)
            holding[i] = holding[i] + more
            spare = spare - more
    return np.array([most] + holding)


def uneven(key, number_of, total, bound, slope):
    if number_of == 2:
        one = jax.random.randint(key, (), max(1, total - bound), min(bound, total - 1) + 1)
        return jnp.stack([one, total - one])
    lengths = jnp.asarray(length_profile(number_of, total, bound, slope), jnp.int32)
    twos = (number_of - 1) // 2
    donor, sink = lengths[1:1 + 2 * twos:2], lengths[2:2 + 2 * twos:2]
    slack = jnp.minimum(donor - 1, bound - sink)
    passed = jax.random.randint(jax.random.fold_in(key, 1), (twos,), 0, 1 << 20) % (slack + 1)
    lengths = lengths.at[1:1 + 2 * twos:2].set(donor - passed).at[2:2 + 2 * twos:2].set(sink + passed)
    return lengths[jax.random.permutation(jax.random.fold_in(key, 2), number_of)]


def setup_inputs(seed: int = 0) -> dict:
    key_list = jax.random.split(jax.random.key(seed), 4)
    queries = draw_queries(jax.random.fold_in(key_list[3], 71), 0)
    keys = draw_keys(jax.random.fold_in(key_list[3], 71), 0)
    doc_ids = jnp.searchsorted(jnp.cumsum(uneven(key_list[2], DOCS, TOKENS, DOC_MOST, 2)), jnp.arange(TOKENS), side="right").astype(jnp.int32)
    return dict(queries=queries, keys=keys, doc_ids=doc_ids)


MASKED_SCORE = -1e+30

def window_columns(query_heads, query_tags, window_keys, window_tags, block_len):
    slot_count, shard_len = window_tags.shape
    groups, per_group, head_dim = (query_heads.shape[1], query_heads.shape[2], query_heads.shape[3])
    score_scale = 1.0 / math.sqrt(head_dim)
    key_offsets = jnp.arange(shard_len, dtype=jnp.int32)
    slot_ids = jnp.arange(slot_count, dtype=jnp.int32)
    query_float = query_heads.astype(jnp.float32)
    keys_float = window_keys.astype(jnp.float32)

    def one_block(totals, block_id):
        first_row = (block_id * block_len).astype(jnp.int32)
        query_block = lax.dynamic_slice_in_dim(query_float, first_row, block_len, 0)
        tags_block = lax.dynamic_slice_in_dim(query_tags, first_row, block_len, 0)
        query_position = (slot_count - 1) * shard_len + first_row + jnp.arange(block_len, dtype=jnp.int32)

        def allowed_of(key_tags, slot_id):
            key_position = slot_id * shard_len + key_offsets
            return (key_tags[None, :] == tags_block[:, None]) & (key_position[None, :] <= query_position[:, None])

        def live_of(key_tags, slot_id):
            highest = jnp.max(key_tags)
            lowest = jnp.min(jnp.where(key_tags > 0, key_tags, jnp.int32(2 ** 30)))
            return (highest >= jnp.min(tags_block)) & (lowest <= jnp.max(tags_block)) & (slot_id * shard_len <= query_position[-1])

        def scores_of(key_slot):
            return jnp.einsum('tgqd,kgd->gqtk', query_block, key_slot) * score_scale

        def stat_step(carried, slot_item):
            key_slot, key_tags, slot_id = slot_item

            def compute(running):
                run_max, run_total = running
                allowed = allowed_of(key_tags, slot_id)
                scores = jnp.where(allowed, scores_of(key_slot), MASKED_SCORE)
                new_max = jnp.maximum(run_max, lax.optimization_barrier(jnp.max(scores, axis=-1)))
                weights = jnp.where(allowed, jnp.exp(scores - new_max[..., None]), 0.0)
                return (new_max, run_total * jnp.exp(run_max - new_max) + lax.optimization_barrier(jnp.sum(weights, axis=-1)))
            return (lax.cond(live_of(key_tags, slot_id), compute, lambda running: running, carried), None)
        start_stats = (jnp.full((groups, per_group, block_len), MASKED_SCORE, jnp.float32), jnp.zeros((groups, per_group, block_len), jnp.float32))
        (row_max, row_total), _ = lax.scan(stat_step, start_stats, (keys_float, window_tags, slot_ids))

        def col_step(carried, slot_item):
            key_slot, key_tags, slot_id = slot_item

            def compute(unused):
                allowed = allowed_of(key_tags, slot_id)
                scores = jnp.where(allowed, scores_of(key_slot), MASKED_SCORE)
                probabilities = jnp.where(allowed, jnp.exp(scores - row_max[..., None]) / row_total[..., None], 0.0)
                return lax.optimization_barrier(jnp.sum(probabilities, axis=2))

            def skip(unused):
                return jnp.zeros((groups, per_group, shard_len), jnp.float32)
            return (carried, lax.cond(live_of(key_tags, slot_id), compute, skip, 0))
        _, partials = lax.scan(col_step, 0, (keys_float, window_tags, slot_ids))
        return (totals + partials, None)
    start_totals = jnp.zeros((slot_count, groups, per_group, shard_len), jnp.float32)
    totals, _ = lax.scan(one_block, start_totals, jnp.arange(query_heads.shape[0] // block_len, dtype=jnp.int32))
    return totals

def reference(queries, keys, doc_ids):
    token_count = queries.shape[0]
    lead_rows = (REACH_DEV - 1) * TOK_DEV
    per_group = QH // KVH
    query_heads = queries.reshape(token_count // TOK_DEV, TOK_DEV, KVH, per_group, HD)
    padded_keys = jnp.concatenate([jnp.zeros((lead_rows, KVH * HD), keys.dtype), keys], 0).reshape(lead_rows + token_count, KVH, HD)
    tags = (doc_ids + 1).astype(jnp.int32)
    padded_tags = jnp.concatenate([jnp.zeros((lead_rows,), jnp.int32), tags], 0)

    def shard_step(columns, shard_id):
        first_row = (shard_id * TOK_DEV).astype(jnp.int32)
        window_keys = lax.dynamic_slice_in_dim(padded_keys, first_row, REACH_DEV * TOK_DEV, 0).reshape(REACH_DEV, TOK_DEV, KVH, HD)
        window_tags = lax.dynamic_slice_in_dim(padded_tags, first_row, REACH_DEV * TOK_DEV, 0).reshape(REACH_DEV, TOK_DEV)
        query_tags = lax.dynamic_slice_in_dim(tags, first_row, TOK_DEV, 0)
        partials = window_columns(query_heads[shard_id], query_tags, window_keys, window_tags, TOK_DEV)
        spread = jnp.moveaxis(partials, 0, 2).reshape(KVH, per_group, REACH_DEV * TOK_DEV)
        current = lax.dynamic_slice_in_dim(columns, first_row, REACH_DEV * TOK_DEV, 2)
        return (lax.dynamic_update_slice_in_dim(columns, current + spread, first_row, 2), None)
    columns = jnp.zeros((KVH, per_group, lead_rows + token_count), jnp.float32)
    columns, _ = lax.scan(shard_step, columns, jnp.arange(token_count // TOK_DEV, dtype=jnp.int32))
    return columns[:, :, lead_rows:].reshape(QH, token_count)
```

```python
import functools
import math

import jax
import jax.numpy as jnp
from jax import lax
from jax.experimental import pallas as pl
from jax.experimental.pallas import tpu as pltpu
from jax.sharding import PartitionSpec as P

HD = 128
QPG = 5
REACH_DEV = 8
MASKED_SCORE = -1e30
ALLOWED_CAP = 3e38
EXP2_SCALE = math.log2(math.e) / math.sqrt(HD)


def score_kernel(own_ref, q_ref, k_ref, qtag_ref, ktag_ref, out_ref, s_ref, cap_ref):
    rows = q_ref.shape[0]
    heads = q_ref.shape[1] // HD
    slots, _, block = ktag_ref.shape
    own = own_ref[0]
    first_tag = jnp.min(qtag_ref[...])
    ahead = jnp.sum(jnp.where(ktag_ref[...] < first_tag, 1.0, 0.0))
    lo = ahead.astype(jnp.int32) // block
    hi = own + 1
    out_ref[...] = jnp.zeros_like(out_ref)

    row_pos = own * block + lax.broadcasted_iota(jnp.int32, (rows, block), 0)
    col_off = lax.broadcasted_iota(jnp.int32, (rows, block), 1)

    @pl.loop(lo, hi)
    def _(c):
        allowed = (ktag_ref[c] == qtag_ref[...]) & (col_off + c * block <= row_pos)
        cap_ref[c] = jnp.where(allowed, ALLOWED_CAP, MASKED_SCORE)

    def lanes(x, op):
        parts = [x[:, i * HD:(i + 1) * HD] for i in range(block // HD)]
        return functools.reduce(op, parts)

    @pl.loop(0, heads)
    def _(h):
        g = h // QPG
        q = q_ref[:, pl.ds(pl.multiple_of(h * HD, HD), HD)]

        def score_step(c, top):
            k = k_ref[pl.ds(pl.multiple_of(c * block, block), block),
                      pl.ds(pl.multiple_of(g * HD, HD), HD)]
            s = lax.dot_general(q, k, (((1,), (1,)), ((), ())), preferred_element_type=jnp.float32)
            s = jnp.minimum(s, cap_ref[c])
            s_ref[c] = s
            return jnp.maximum(top, lanes(s, jnp.maximum))

        top = lax.fori_loop(lo, hi, score_step, jnp.full((rows, HD), MASKED_SCORE, jnp.float32))
        row_max = jnp.max(top, axis=-1, keepdims=True)

        def exp_step(c, total):
            e = jnp.exp2((s_ref[c] - row_max) * EXP2_SCALE)
            s_ref[c] = e
            return total + lanes(e, jnp.add)

        total = lax.fori_loop(lo, hi, exp_step, jnp.zeros((rows, HD), jnp.float32))
        inv = 1.0 / jnp.sum(total, axis=-1, keepdims=True)

        @pl.loop(lo, hi)
        def _(c):
            out_ref[c, pl.ds(h, 1), :] = jnp.sum(s_ref[c] * inv, axis=0, keepdims=True)


def window_columns(own, q, k, qtag, ktag):
    rows = q.shape[0]
    heads = q.shape[1] // HD
    slots, _, block = ktag.shape
    vmem = pl.BlockSpec(memory_space=pltpu.VMEM)
    return pl.pallas_call(
        score_kernel,
        out_shape=jax.ShapeDtypeStruct((slots, heads, block), jnp.float32),
        in_specs=[pl.BlockSpec(memory_space=pltpu.SMEM), vmem, vmem, vmem, vmem],
        out_specs=vmem,
        scratch_shapes=[
            pltpu.VMEM((slots, rows, block), jnp.float32),
            pltpu.VMEM((slots, rows, block), jnp.float32),
        ],
        compiler_params=pltpu.CompilerParams(vmem_limit_bytes=50 * 1024 * 1024),
    )(own, q, k, qtag, ktag)


def body(queries, keys, doc_ids):
    q = lax.all_to_all(queries, "kvh", split_axis=1, concat_axis=0, tiled=True)
    k = lax.all_to_all(keys, "kvh", split_axis=1, concat_axis=0, tiled=True)
    peers = lax.axis_size("seq")
    me = lax.axis_index("seq")
    shard_len = q.shape[0]
    slots = min(REACH_DEV, peers)
    start = jnp.maximum(me - (slots - 1), 0)
    own = me - start
    tags = doc_ids + 1
    all_keys = lax.all_gather(k, "seq", axis=0, tiled=True)
    all_tags = lax.all_gather(tags, "seq", axis=0, tiled=False)
    if peers > slots:
        all_keys = lax.dynamic_slice_in_dim(all_keys, start * shard_len, slots * shard_len, 0)
        all_tags = lax.dynamic_slice_in_dim(all_tags, start, slots, 0)
    partials = window_columns(own.reshape(1), q, all_keys, tags.reshape(shard_len, 1),
                              all_tags.reshape(slots, 1, shard_len))
    if peers > slots:
        spread = jnp.zeros((peers,) + partials.shape[1:], jnp.float32)
        partials = lax.dynamic_update_slice_in_dim(spread, partials, start, 0)
    back = lax.all_to_all(partials, "seq", split_axis=0, concat_axis=0, tiled=True)
    return jnp.sum(back, axis=0)


def solution(mesh):
    in_specs = (P(("seq", "kvh"), None), P(("seq", "kvh"), None), P("seq"))
    out_specs = P("kvh", "seq")
    return jax.shard_map(body, mesh=mesh, in_specs=in_specs, out_specs=out_specs, check_vma=False)
```

```python
import functools
import math

import jax
import jax.numpy as jnp
from jax import lax
from jax.experimental import pallas as pl
from jax.experimental.pallas import tpu as pltpu
from jax.sharding import PartitionSpec as P

HD = 128
QPG = 5
REACH_DEV = 8
MASKED_SCORE = -1e30
ALLOWED_CAP = 3e38
EXP2_SCALE = math.log2(math.e) / math.sqrt(HD)


def score_kernel(own_ref, q_ref, k_ref, qtag_ref, ktag_ref, out_ref, s_ref, cap_ref):
    rows = q_ref.shape[0]
    heads = q_ref.shape[1] // HD
    slots, _, block = ktag_ref.shape
    own = own_ref[0]
    first_tag = jnp.min(qtag_ref[...])
    ahead = jnp.sum(jnp.where(ktag_ref[...] < first_tag, 1.0, 0.0))
    lo = ahead.astype(jnp.int32) // block
    hi = own + 1
    out_ref[...] = jnp.zeros_like(out_ref)

    row_pos = own * block + lax.broadcasted_iota(jnp.int32, (rows, block), 0)
    col_off = lax.broadcasted_iota(jnp.int32, (rows, block), 1)

    @pl.loop(lo, hi)
    def _(c):
        allowed = (ktag_ref[c] == qtag_ref[...]) & (col_off + c * block <= row_pos)
        cap_ref[c] = jnp.where(allowed, ALLOWED_CAP, MASKED_SCORE)

    def lanes(x, op):
        parts = [x[:, i * HD:(i + 1) * HD] for i in range(block // HD)]
        return functools.reduce(op, parts)

    @pl.loop(0, heads)
    def _(h):
        g = h // QPG
        q = q_ref[:, pl.ds(pl.multiple_of(h * HD, HD), HD)]

        def score_step(c, top):
            k = k_ref[pl.ds(pl.multiple_of(c * block, block), block),
                      pl.ds(pl.multiple_of(g * HD, HD), HD)]
            s = lax.dot_general(q, k, (((1,), (1,)), ((), ())), preferred_element_type=jnp.float32)
            s = jnp.minimum(s, cap_ref[c])
            s_ref[c] = s
            return jnp.maximum(top, lanes(s, jnp.maximum))

        top = lax.fori_loop(lo, hi, score_step, jnp.full((rows, HD), MASKED_SCORE, jnp.float32))
        row_max = jnp.max(top, axis=-1, keepdims=True)

        def exp_step(c, total):
            e = jnp.exp2((s_ref[c] - row_max) * EXP2_SCALE)
            s_ref[c] = e
            return total + lanes(e, jnp.add)

        total = lax.fori_loop(lo, hi, exp_step, jnp.zeros((rows, HD), jnp.float32))
        inv = 1.0 / jnp.sum(total, axis=-1, keepdims=True)

        @pl.loop(lo, hi)
        def _(c):
            out_ref[c, pl.ds(h, 1), :] = jnp.sum(s_ref[c] * inv, axis=0, keepdims=True)


def window_columns(own, q, k, qtag, ktag):
    rows = q.shape[0]
    heads = q.shape[1] // HD
    slots, _, block = ktag.shape
    vmem = pl.BlockSpec(memory_space=pltpu.VMEM)
    return pl.pallas_call(
        score_kernel,
        out_shape=jax.ShapeDtypeStruct((slots, heads, block), jnp.float32),
        in_specs=[pl.BlockSpec(memory_space=pltpu.SMEM), vmem, vmem, vmem, vmem],
        out_specs=vmem,
        scratch_shapes=[
            pltpu.VMEM((slots, rows, block), jnp.float32),
            pltpu.VMEM((slots, rows, block), jnp.float32),
        ],
        compiler_params=pltpu.CompilerParams(vmem_limit_bytes=50 * 1024 * 1024),
    )(own, q, k, qtag, ktag)


def hop(src, dst, send_sem, recv_sem, device_id):
    return pltpu.make_async_remote_copy(
        src_ref=src, dst_ref=dst, send_sem=send_sem, recv_sem=recv_sem,
        device_id=device_id, device_id_type=pl.DeviceIdType.MESH)


def meet(seq_peers, kvh_peers):
    barrier = pltpu.get_barrier_semaphore()
    me, kv = lax.axis_index("seq"), lax.axis_index("kvh")
    for i in range(1, seq_peers):
        pl.semaphore_signal(barrier, inc=1, device_id={"seq": lax.rem(me + i, seq_peers)},
                            device_id_type=pl.DeviceIdType.MESH)
    for i in range(1, kvh_peers):
        pl.semaphore_signal(barrier, inc=1, device_id={"kvh": lax.rem(kv + i, kvh_peers)},
                            device_id_type=pl.DeviceIdType.MESH)
    pl.semaphore_wait(barrier, seq_peers + kvh_peers - 2)


def gather_kernel(peers, groups, q_ref, k_ref, tag_ref, q_out, k_out, tag_out,
                  own_sem, kg_send, kg_recv, qg_send, qg_recv, tag_send, tag_recv,
                  z_send, x_send, k_recv):
    me, kv = lax.axis_index("seq"), lax.axis_index("kvh")
    z, x = me // 2, lax.rem(me, 2)
    z_count = peers // 2
    part = q_ref.shape[0]
    q_cols, k_cols = q_out.shape[1], k_out.shape[2]
    meet(peers, groups)

    rows = pl.ds(pl.multiple_of(kv * part, part), part)

    def q_of(g):
        return q_ref.at[:, pl.ds(pl.multiple_of(g * q_cols, q_cols), q_cols)]

    def k_of(g):
        return k_ref.at[:, pl.ds(pl.multiple_of(g * k_cols, k_cols), k_cols)]

    k_sends, q_sends, tag_sends = [], [], []
    for i in range(1, groups):
        to = lax.rem(kv + i, groups)
        k_sends.append(hop(k_of(to), k_out.at[me, rows], kg_send.at[i], kg_recv.at[i], {"kvh": to}))
        q_sends.append(hop(q_of(to), q_out.at[rows], qg_send.at[i], qg_recv.at[i], {"kvh": to}))
    for i in range(1, peers):
        to = lax.rem(me + i, peers)
        tag_sends.append(hop(tag_ref, tag_out.at[me], tag_send.at[i], tag_recv.at[i], {"seq": to}))
    local = [pltpu.make_async_copy(k_of(kv), k_out.at[me, rows], own_sem.at[0]),
             pltpu.make_async_copy(q_of(kv), q_out.at[rows], own_sem.at[1]),
             pltpu.make_async_copy(tag_ref, tag_out.at[me], own_sem.at[2])]
    for copy in k_sends + local[:1] + q_sends + local[1:] + tag_sends:
        copy.start()
    local[0].wait()
    for copy in k_sends:
        copy.wait_recv()

    def along_z(b):
        return hop(k_out.at[b], k_out.at[b], z_send.at[b], k_recv.at[b], {"seq": me + 2})

    def across_x(b):
        return hop(k_out.at[b], k_out.at[b], x_send.at[b], k_recv.at[b], {"seq": me + 1 - 2 * x})

    for d in range(z_count):
        b = me - 2 * d

        @pl.when(z >= d)
        def _():
            if d > 0:
                along_z(b).wait_recv()

            @pl.when(z < z_count - 1)
            def _():
                along_z(b).start()

            @pl.when((x == 0) | (d > 0))
            def _():
                across_x(b).start()

    for d in range(z_count):
        b = me - 2 * d
        other = b + 1 - 2 * x

        @pl.when((z >= d) & ((x == 1) | (d > 0)))
        def _():
            across_x(other).wait_recv()

        @pl.when((z >= d) & (z < z_count - 1))
        def _():
            along_z(b).wait_send()

        @pl.when((z >= d) & ((x == 0) | (d > 0)))
        def _():
            across_x(b).wait_send()

    for copy in k_sends:
        copy.wait_send()
    for copy in local[1:]:
        copy.wait()
    for copy in q_sends + tag_sends:
        copy.wait()


def gathered(queries, keys, tags):
    peers, groups = lax.axis_size("seq"), lax.axis_size("kvh")
    part = queries.shape[0]
    anywhere = pl.BlockSpec(memory_space=pl.ANY)
    dma = pltpu.SemaphoreType.DMA
    return pl.pallas_call(
        functools.partial(gather_kernel, peers, groups),
        out_shape=(
            jax.ShapeDtypeStruct((part * groups, queries.shape[1] // groups), queries.dtype),
            jax.ShapeDtypeStruct((peers, part * groups, keys.shape[1] // groups), keys.dtype),
            jax.ShapeDtypeStruct((peers, 1, tags.shape[1]), tags.dtype),
        ),
        in_specs=[anywhere] * 3,
        out_specs=(anywhere,) * 3,
        scratch_shapes=[dma((3,)), dma((groups,)), dma((groups,)), dma((groups,)), dma((groups,)),
                        dma((peers,)), dma((peers,)), dma((peers,)), dma((peers,)), dma((peers,))],
        compiler_params=pltpu.CompilerParams(collective_id=0, has_side_effects=True),
    )(queries, keys, tags)


def return_kernel(peers, part_ref, out_ref, got, send_sem, recv_sem):
    me = lax.axis_index("seq")
    meet(peers, 1)

    def send(to):
        return hop(part_ref.at[to], got.at[me], send_sem.at[to], recv_sem.at[me], {"seq": to})

    def arrival(i):
        return hop(part_ref.at[i], got.at[i], send_sem.at[i], recv_sem.at[i], {"seq": i})

    for j in range(peers):
        @pl.when(j < me)
        def _():
            send(j).start()
    out_ref[...] = part_ref[me]
    for i in range(peers):
        @pl.when(i > me)
        def _():
            arrival(i).wait_recv()
            out_ref[...] += got[i]
    for j in range(peers):
        @pl.when(j < me)
        def _():
            send(j).wait_send()


def returned(partials):
    peers = lax.axis_size("seq")
    vmem = pl.BlockSpec(memory_space=pltpu.VMEM)
    dma = pltpu.SemaphoreType.DMA
    return pl.pallas_call(
        functools.partial(return_kernel, peers),
        out_shape=jax.ShapeDtypeStruct(partials.shape[1:], partials.dtype),
        in_specs=[vmem],
        out_specs=vmem,
        scratch_shapes=[pltpu.VMEM(partials.shape, partials.dtype), dma((peers,)), dma((peers,))],
        compiler_params=pltpu.CompilerParams(collective_id=1, has_side_effects=True),
    )(partials)


def reach_body(queries, keys, doc_ids):
    tags = (doc_ids + 1).reshape(1, -1)
    shard_len = tags.shape[1]
    q, k, all_tags = gathered(queries, keys, tags)
    own = lax.axis_index("seq").reshape(1)
    partials = window_columns(own, q, k.reshape(-1, k.shape[2]), tags.reshape(shard_len, 1), all_tags)
    return returned(partials)


def body(queries, keys, doc_ids):
    q = lax.all_to_all(queries, "kvh", split_axis=1, concat_axis=0, tiled=True)
    k = lax.all_to_all(keys, "kvh", split_axis=1, concat_axis=0, tiled=True)
    peers = lax.axis_size("seq")
    me = lax.axis_index("seq")
    shard_len = q.shape[0]
    slots = min(REACH_DEV, peers)
    start = jnp.maximum(me - (slots - 1), 0)
    own = me - start
    tags = doc_ids + 1
    all_keys = lax.all_gather(k, "seq", axis=0, tiled=True)
    all_tags = lax.all_gather(tags, "seq", axis=0, tiled=False)
    if peers > slots:
        all_keys = lax.dynamic_slice_in_dim(all_keys, start * shard_len, slots * shard_len, 0)
        all_tags = lax.dynamic_slice_in_dim(all_tags, start, slots, 0)
    partials = window_columns(own.reshape(1), q, all_keys, tags.reshape(shard_len, 1),
                              all_tags.reshape(slots, 1, shard_len))
    if peers > slots:
        spread = jnp.zeros((peers,) + partials.shape[1:], jnp.float32)
        partials = lax.dynamic_update_slice_in_dim(spread, partials, start, 0)
    back = lax.all_to_all(partials, "seq", split_axis=0, concat_axis=0, tiled=True)
    return jnp.sum(back, axis=0)


def solution(mesh):
    in_specs = (P(("seq", "kvh"), None), P(("seq", "kvh"), None), P("seq"))
    out_specs = P("kvh", "seq")
    whole_reach = mesh.shape["seq"] == REACH_DEV
    part = reach_body if whole_reach else body
    return jax.shard_map(part, mesh=mesh, in_specs=in_specs, out_specs=out_specs, check_vma=False)
```

```python
import functools
import math

import jax
import jax.numpy as jnp
from jax import lax
from jax.experimental import pallas as pl
from jax.experimental.pallas import tpu as pltpu
from jax.sharding import PartitionSpec as P

HD = 128
QPG = 5
REACH_DEV = 8
TILE = 512
STEP = 32
MASKED_SCORE = -1e30
ALLOWED_CAP = 3e38
EXP2_SCALE = math.log2(math.e) / math.sqrt(HD)


def score_kernel(own_ref, q_ref, k_ref, qtag_ref, ktag_ref, out_ref,
                 s0_ref, s1_ref, s2_ref, cap_ref, top_ref, max_ref, total_ref, inv_ref):
    rows = q_ref.shape[0]
    heads = q_ref.shape[1] // HD
    slots, _, block = ktag_ref.shape
    s_refs = (s0_ref, s1_ref, s2_ref)
    tile = s0_ref.shape[1]
    tiles = rows // tile
    units = heads * tiles
    own = own_ref[0]
    first_tag = jnp.min(qtag_ref[...])
    slot_of = lax.broadcasted_iota(jnp.int32, ktag_ref.shape, 0)
    ahead = jnp.sum(jnp.where((ktag_ref[...] < first_tag) & (slot_of < own), 1.0, 0.0))
    lo = ahead.astype(jnp.int32) // block
    hi = own + 1
    out_ref[...] = jnp.zeros_like(out_ref)

    row_pos = own * block + lax.broadcasted_iota(jnp.int32, (rows, block), 0)
    col_off = lax.broadcasted_iota(jnp.int32, (rows, block), 1)

    @pl.loop(lo, hi)
    def _(c):
        allowed = (ktag_ref[c] == qtag_ref[...]) & (col_off + c * block <= row_pos)
        cap_ref[c] = jnp.where(allowed, ALLOWED_CAP, MASKED_SCORE)

    def lane_tiles(x):
        return [x[:, i * HD:(i + 1) * HD] for i in range(block // HD)]

    def score_step(u, c):
        h, t = u // tiles, u % tiles
        first = t * tile
        q = q_ref[first:first + tile, h * HD:(h + 1) * HD]
        k = k_ref[pl.ds(pl.multiple_of(c * block, block), block),
                  h // QPG * HD:(h // QPG + 1) * HD]
        s_ref = s_refs[u % 3]
        s = lax.dot_general(q, k, (((1,), (1,)), ((), ())), preferred_element_type=jnp.float32)
        for r in range(0, tile, STEP):
            here = jnp.minimum(s[r:r + STEP], cap_ref[c, first + r:first + r + STEP, :])
            s_ref[c, r:r + STEP] = here
            top_ref[r:r + STEP] = functools.reduce(jnp.maximum, lane_tiles(here), top_ref[r:r + STEP])

    def exp_step(u, c):
        s_ref = s_refs[u % 3]
        for r in range(0, tile, STEP):
            row_max = max_ref[r:r + STEP]
            total = total_ref[r:r + STEP]
            for i in range(block // HD):
                cols = slice(i * HD, (i + 1) * HD)
                e = jnp.exp2((s_ref[c, r:r + STEP, cols] - row_max) * EXP2_SCALE)
                s_ref[c, r:r + STEP, cols] = e
                total = total + e
            total_ref[r:r + STEP] = total

    def column_step(u, c):
        s_ref = s_refs[u % 3]
        sums = [jnp.zeros((8, HD), jnp.float32)] * (block // HD)
        for r in range(0, tile, 8):
            inv = inv_ref[r:r + 8]
            sums = [acc + s_ref[c, r:r + 8, i * HD:(i + 1) * HD] * inv
                    for i, acc in enumerate(sums)]
        out_ref[c, u // tiles:u // tiles + 1, :] += jnp.sum(jnp.concatenate(sums, axis=1), axis=0, keepdims=True)

    def turn(u, stages):
        if 0 in stages:
            top_ref[...] = jnp.full(top_ref.shape, MASKED_SCORE, jnp.float32)
        if 1 in stages:
            total_ref[...] = jnp.zeros(total_ref.shape, jnp.float32)

        @pl.loop(lo, hi)
        def _(c):
            if 0 in stages:
                score_step(u, c)
            if 1 in stages:
                exp_step(u - 1, c)
            if 2 in stages:
                column_step(u - 2, c)

        if 0 in stages:
            row_max = jnp.max(top_ref[...], axis=-1, keepdims=True)
            max_ref[...] = jnp.broadcast_to(row_max, max_ref.shape)
        if 1 in stages:
            inv = 1.0 / jnp.sum(total_ref[...], axis=-1, keepdims=True)
            inv_ref[...] = jnp.broadcast_to(inv, inv_ref.shape)

    for u in range(units + 2):
        turn(u, [i for i in range(3) if 0 <= u - i < units])


def window_columns(own, q, k, qtag, ktag):
    rows = q.shape[0]
    heads = q.shape[1] // HD
    slots, _, block = ktag.shape
    vmem = pl.BlockSpec(memory_space=pltpu.VMEM)
    return pl.pallas_call(
        score_kernel,
        out_shape=jax.ShapeDtypeStruct((slots, heads, block), jnp.float32),
        in_specs=[pl.BlockSpec(memory_space=pltpu.SMEM), vmem, vmem, vmem, vmem],
        out_specs=vmem,
        scratch_shapes=[pltpu.VMEM((slots, TILE, block), jnp.float32)] * 3 + [
            pltpu.VMEM((slots, rows, block), jnp.float32),
        ] + [pltpu.VMEM((TILE, HD), jnp.float32)] * 4,
        compiler_params=pltpu.CompilerParams(vmem_limit_bytes=50 * 1024 * 1024),
    )(own, q, k, qtag, ktag)


def hop(src, dst, send_sem, recv_sem, device_id):
    return pltpu.make_async_remote_copy(
        src_ref=src, dst_ref=dst, send_sem=send_sem, recv_sem=recv_sem,
        device_id=device_id, device_id_type=pl.DeviceIdType.MESH)


def meet(seq_peers, kvh_peers):
    barrier = pltpu.get_barrier_semaphore()
    me, kv = lax.axis_index("seq"), lax.axis_index("kvh")
    for i in range(1, seq_peers):
        pl.semaphore_signal(barrier, inc=1, device_id={"seq": lax.rem(me + i, seq_peers)},
                            device_id_type=pl.DeviceIdType.MESH)
    for i in range(1, kvh_peers):
        pl.semaphore_signal(barrier, inc=1, device_id={"kvh": lax.rem(kv + i, kvh_peers)},
                            device_id_type=pl.DeviceIdType.MESH)
    pl.semaphore_wait(barrier, seq_peers + kvh_peers - 2)


def gather_kernel(peers, groups, q_ref, k_ref, tag_ref, q_out, k_out, tag_out,
                  own_sem, kg_send, kg_recv, qg_send, qg_recv, tag_send, tag_recv,
                  z_send, x_send, k_recv):
    me, kv = lax.axis_index("seq"), lax.axis_index("kvh")
    z, x = me // 2, lax.rem(me, 2)
    z_count = peers // 2
    part = q_ref.shape[0]
    q_cols, k_cols = q_out.shape[1], k_out.shape[2]
    meet(peers, groups)

    rows = pl.ds(pl.multiple_of(kv * part, part), part)

    def q_of(g):
        return q_ref.at[:, pl.ds(pl.multiple_of(g * q_cols, q_cols), q_cols)]

    def k_of(g):
        return k_ref.at[:, pl.ds(pl.multiple_of(g * k_cols, k_cols), k_cols)]

    k_sends, q_sends, tag_sends = [], [], []
    for i in range(1, groups):
        to = lax.rem(kv + i, groups)
        k_sends.append(hop(k_of(to), k_out.at[me, rows], kg_send.at[i], kg_recv.at[i], {"kvh": to}))
        q_sends.append(hop(q_of(to), q_out.at[rows], qg_send.at[i], qg_recv.at[i], {"kvh": to}))
    for i in range(1, peers):
        to = lax.rem(me + i, peers)
        tag_sends.append(hop(tag_ref, tag_out.at[me], tag_send.at[i], tag_recv.at[i], {"seq": to}))
    local = [pltpu.make_async_copy(k_of(kv), k_out.at[me, rows], own_sem.at[0]),
             pltpu.make_async_copy(q_of(kv), q_out.at[rows], own_sem.at[1]),
             pltpu.make_async_copy(tag_ref, tag_out.at[me], own_sem.at[2])]
    for copy in k_sends + local:
        copy.start()
    local[0].wait()
    for copy in k_sends:
        copy.wait_recv()

    def along_z(b):
        return hop(k_out.at[b], k_out.at[b], z_send.at[b], k_recv.at[b], {"seq": me + 2})

    def across_x(b):
        return hop(k_out.at[b], k_out.at[b], x_send.at[b], k_recv.at[b], {"seq": me + 1 - 2 * x})

    for d in range(z_count):
        b = me - 2 * d
        if d == 1:
            for copy in q_sends + tag_sends:
                copy.start()

        @pl.when(z >= d)
        def _():
            if d > 0:
                along_z(b).wait_recv()

            @pl.when(z < z_count - 1)
            def _():
                along_z(b).start()

            @pl.when((x == 0) | (d > 0))
            def _():
                across_x(b).start()

    for d in range(z_count):
        b = me - 2 * d
        other = b + 1 - 2 * x

        @pl.when((z >= d) & ((x == 1) | (d > 0)))
        def _():
            across_x(other).wait_recv()

        @pl.when((z >= d) & (z < z_count - 1))
        def _():
            along_z(b).wait_send()

        @pl.when((z >= d) & ((x == 0) | (d > 0)))
        def _():
            across_x(b).wait_send()

    for copy in k_sends:
        copy.wait_send()
    for copy in local[1:]:
        copy.wait()
    for copy in q_sends + tag_sends:
        copy.wait()


def gathered(queries, keys, tags):
    peers, groups = lax.axis_size("seq"), lax.axis_size("kvh")
    part = queries.shape[0]
    anywhere = pl.BlockSpec(memory_space=pl.ANY)
    dma = pltpu.SemaphoreType.DMA
    return pl.pallas_call(
        functools.partial(gather_kernel, peers, groups),
        out_shape=(
            jax.ShapeDtypeStruct((part * groups, queries.shape[1] // groups), queries.dtype),
            jax.ShapeDtypeStruct((peers, part * groups, keys.shape[1] // groups), keys.dtype),
            jax.ShapeDtypeStruct((peers, 1, tags.shape[1]), tags.dtype),
        ),
        in_specs=[anywhere] * 3,
        out_specs=(pl.BlockSpec(memory_space=pltpu.VMEM),) * 3,
        scratch_shapes=[dma((3,)), dma((groups,)), dma((groups,)), dma((groups,)), dma((groups,)),
                        dma((peers,)), dma((peers,)), dma((peers,)), dma((peers,)), dma((peers,))],
        compiler_params=pltpu.CompilerParams(collective_id=0, has_side_effects=True),
    )(queries, keys, tags)


def return_kernel(peers, part_ref, out_ref, got, send_sem, recv_sem):
    me = lax.axis_index("seq")
    meet(peers, 1)

    def send(to):
        return hop(part_ref.at[to], got.at[me], send_sem.at[to], recv_sem.at[me], {"seq": to})

    def arrival(i):
        return hop(part_ref.at[i], got.at[i], send_sem.at[i], recv_sem.at[i], {"seq": i})

    for j in range(peers):
        @pl.when(j < me)
        def _():
            send(j).start()
    out_ref[...] = part_ref[me]
    for i in range(peers):
        @pl.when(i > me)
        def _():
            arrival(i).wait_recv()
            out_ref[...] += got[i]
    for j in range(peers):
        @pl.when(j < me)
        def _():
            send(j).wait_send()


def returned(partials):
    peers = lax.axis_size("seq")
    vmem = pl.BlockSpec(memory_space=pltpu.VMEM)
    dma = pltpu.SemaphoreType.DMA
    return pl.pallas_call(
        functools.partial(return_kernel, peers),
        out_shape=jax.ShapeDtypeStruct(partials.shape[1:], partials.dtype),
        in_specs=[vmem],
        out_specs=vmem,
        scratch_shapes=[pltpu.VMEM(partials.shape, partials.dtype), dma((peers,)), dma((peers,))],
        compiler_params=pltpu.CompilerParams(collective_id=1, has_side_effects=True),
    )(partials)


def reach_body(queries, keys, doc_ids):
    tags = (doc_ids + 1).reshape(1, -1)
    shard_len = tags.shape[1]
    q, k, all_tags = gathered(queries, keys, tags)
    own = lax.axis_index("seq").reshape(1)
    partials = window_columns(own, q, k.reshape(-1, k.shape[2]), tags.reshape(shard_len, 1), all_tags)
    return returned(partials)


def body(queries, keys, doc_ids):
    q = lax.all_to_all(queries, "kvh", split_axis=1, concat_axis=0, tiled=True)
    k = lax.all_to_all(keys, "kvh", split_axis=1, concat_axis=0, tiled=True)
    peers = lax.axis_size("seq")
    me = lax.axis_index("seq")
    shard_len = q.shape[0]
    slots = min(REACH_DEV, peers)
    start = jnp.maximum(me - (slots - 1), 0)
    own = me - start
    tags = doc_ids + 1
    all_keys = lax.all_gather(k, "seq", axis=0, tiled=True)
    all_tags = lax.all_gather(tags, "seq", axis=0, tiled=False)
    if peers > slots:
        all_keys = lax.dynamic_slice_in_dim(all_keys, start * shard_len, slots * shard_len, 0)
        all_tags = lax.dynamic_slice_in_dim(all_tags, start, slots, 0)
    partials = window_columns(own.reshape(1), q, all_keys, tags.reshape(shard_len, 1),
                              all_tags.reshape(slots, 1, shard_len))
    if peers > slots:
        spread = jnp.zeros((peers,) + partials.shape[1:], jnp.float32)
        partials = lax.dynamic_update_slice_in_dim(spread, partials, start, 0)
    back = lax.all_to_all(partials, "seq", split_axis=0, concat_axis=0, tiled=True)
    return jnp.sum(back, axis=0)


def solution(mesh):
    in_specs = (P(("seq", "kvh"), None), P(("seq", "kvh"), None), P("seq"))
    out_specs = P("kvh", "seq")
    whole_reach = mesh.shape["seq"] == REACH_DEV
    part = reach_body if whole_reach else body
    return jax.shard_map(part, mesh=mesh, in_specs=in_specs, out_specs=out_specs, check_vma=False)
```

```python
import functools
import math

import jax
import jax.numpy as jnp
from jax import lax
from jax.experimental import pallas as pl
from jax.experimental.pallas import tpu as pltpu
from jax.sharding import PartitionSpec as P

HD = 128
QPG = 5
REACH_DEV = 8
TILE = 512
STEP = 32
MASKED_SCORE = -1e30
ALLOWED_CAP = 3e38
EXP2_SCALE = math.log2(math.e) / math.sqrt(HD)


def score_kernel(own_ref, q_ref, k_ref, qtag_ref, ktag_ref, out_ref,
                 s0_ref, s1_ref, s2_ref, cap_ref, top_ref, max_ref, total_ref, inv_ref):
    rows = q_ref.shape[0]
    heads = q_ref.shape[1] // HD
    slots, _, block = ktag_ref.shape
    s_refs = (s0_ref, s1_ref, s2_ref)
    tile = s0_ref.shape[1]
    tiles = rows // tile
    units = heads * tiles
    own = own_ref[0]
    first_tag = jnp.min(qtag_ref[...])
    slot_of = lax.broadcasted_iota(jnp.int32, ktag_ref.shape, 0)
    ahead = jnp.sum(jnp.where((ktag_ref[...] < first_tag) & (slot_of < own), 1.0, 0.0))
    lo = ahead.astype(jnp.int32) // block
    hi = own + 1
    out_ref[...] = jnp.zeros_like(out_ref)

    row_pos = own * block + lax.broadcasted_iota(jnp.int32, (rows, block), 0)
    col_off = lax.broadcasted_iota(jnp.int32, (rows, block), 1)

    @pl.loop(lo, hi)
    def _(c):
        allowed = (ktag_ref[c] == qtag_ref[...]) & (col_off + c * block <= row_pos)
        cap_ref[c] = jnp.where(allowed, ALLOWED_CAP, MASKED_SCORE)

    def lane_tiles(x):
        return [x[:, i * HD:(i + 1) * HD] for i in range(block // HD)]

    def score_step(u, c):
        h, t = u // tiles, u % tiles
        first = t * tile
        q = q_ref[first:first + tile, h * HD:(h + 1) * HD]
        k = k_ref[pl.ds(pl.multiple_of(c * block, block), block),
                  h // QPG * HD:(h // QPG + 1) * HD]
        s_ref = s_refs[u % 3]
        s = lax.dot_general(q, k, (((1,), (1,)), ((), ())), preferred_element_type=jnp.float32)
        for r in range(0, tile, STEP):
            here = jnp.minimum(s[r:r + STEP], cap_ref[c, first + r:first + r + STEP, :])
            s_ref[c, r:r + STEP] = here
            top_ref[r:r + STEP] = functools.reduce(jnp.maximum, lane_tiles(here), top_ref[r:r + STEP])

    def exp_step(u, c):
        s_ref = s_refs[u % 3]
        for r in range(0, tile, STEP):
            row_max = max_ref[r:r + STEP]
            total = total_ref[r:r + STEP]
            for i in range(block // HD):
                cols = slice(i * HD, (i + 1) * HD)
                e = jnp.exp2((s_ref[c, r:r + STEP, cols] - row_max) * EXP2_SCALE)
                s_ref[c, r:r + STEP, cols] = e
                total = total + e
            total_ref[r:r + STEP] = total

    def column_step(u, c):
        s_ref = s_refs[u % 3]
        sums = [jnp.zeros((8, HD), jnp.float32)] * (block // HD)
        for r in range(0, tile, 8):
            inv = inv_ref[r:r + 8]
            sums = [acc + s_ref[c, r:r + 8, i * HD:(i + 1) * HD] * inv
                    for i, acc in enumerate(sums)]
        out_ref[c, u // tiles:u // tiles + 1, :] += jnp.sum(jnp.concatenate(sums, axis=1), axis=0, keepdims=True)

    def turn(u, stages):
        if 0 in stages:
            top_ref[...] = jnp.full(top_ref.shape, MASKED_SCORE, jnp.float32)
        if 1 in stages:
            total_ref[...] = jnp.zeros(total_ref.shape, jnp.float32)

        @pl.loop(lo, hi)
        def _(c):
            if 0 in stages:
                score_step(u, c)
            if 1 in stages:
                exp_step(u - 1, c)
            if 2 in stages:
                column_step(u - 2, c)

        if 0 in stages:
            row_max = jnp.max(top_ref[...], axis=-1, keepdims=True)
            max_ref[...] = jnp.broadcast_to(row_max, max_ref.shape)
        if 1 in stages:
            inv = 1.0 / jnp.sum(total_ref[...], axis=-1, keepdims=True)
            inv_ref[...] = jnp.broadcast_to(inv, inv_ref.shape)

    for u in range(units + 2):
        turn(u, [i for i in range(3) if 0 <= u - i < units])


def window_columns(own, q, k, qtag, ktag):
    rows = q.shape[0]
    heads = q.shape[1] // HD
    slots, _, block = ktag.shape
    vmem = pl.BlockSpec(memory_space=pltpu.VMEM)
    return pl.pallas_call(
        score_kernel,
        out_shape=jax.ShapeDtypeStruct((slots, heads, block), jnp.float32),
        in_specs=[pl.BlockSpec(memory_space=pltpu.SMEM), vmem, vmem, vmem, vmem],
        out_specs=vmem,
        scratch_shapes=[pltpu.VMEM((slots, TILE, block), jnp.float32)] * 3 + [
            pltpu.VMEM((slots, rows, block), jnp.float32),
        ] + [pltpu.VMEM((TILE, HD), jnp.float32)] * 4,
        compiler_params=pltpu.CompilerParams(vmem_limit_bytes=40 * 1024 * 1024),
    )(own, q, k, qtag, ktag)


def hop(src, dst, send_sem, recv_sem, device_id):
    return pltpu.make_async_remote_copy(
        src_ref=src, dst_ref=dst, send_sem=send_sem, recv_sem=recv_sem,
        device_id=device_id, device_id_type=pl.DeviceIdType.MESH)


def meet(seq_peers, kvh_peers):
    barrier = pltpu.get_barrier_semaphore()
    me, kv = lax.axis_index("seq"), lax.axis_index("kvh")
    for i in range(1, seq_peers):
        pl.semaphore_signal(barrier, inc=1, device_id={"seq": lax.rem(me + i, seq_peers)},
                            device_id_type=pl.DeviceIdType.MESH)
    for i in range(1, kvh_peers):
        pl.semaphore_signal(barrier, inc=1, device_id={"kvh": lax.rem(kv + i, kvh_peers)},
                            device_id_type=pl.DeviceIdType.MESH)
    pl.semaphore_wait(barrier, seq_peers + kvh_peers - 2)


def gather_kernel(peers, groups, q_ref, k_ref, tag_ref, q_out, k_out, tag_out,
                  own_sem, kg_send, kg_recv, qg_send, qg_recv, tag_send, tag_recv,
                  z_send, x_send, k_recv):
    me, kv = lax.axis_index("seq"), lax.axis_index("kvh")
    z, x = me // 2, lax.rem(me, 2)
    z_count = peers // 2
    part = q_ref.shape[0]
    q_cols, k_cols = q_out.shape[1], k_out.shape[2]
    meet(peers, groups)

    rows = pl.ds(pl.multiple_of(kv * part, part), part)

    def q_of(g):
        return q_ref.at[:, pl.ds(pl.multiple_of(g * q_cols, q_cols), q_cols)]

    def k_of(g):
        return k_ref.at[:, pl.ds(pl.multiple_of(g * k_cols, k_cols), k_cols)]

    k_sends, q_sends, tag_sends = [], [], []
    for i in range(1, groups):
        to = lax.rem(kv + i, groups)
        k_sends.append(hop(k_of(to), k_out.at[me, rows], kg_send.at[i], kg_recv.at[i], {"kvh": to}))
        q_sends.append(hop(q_of(to), q_out.at[rows], qg_send.at[i], qg_recv.at[i], {"kvh": to}))
    for i in range(1, peers):
        to = lax.rem(me + i, peers)
        tag_sends.append(hop(tag_ref, tag_out.at[me], tag_send.at[i], tag_recv.at[i], {"seq": to}))
    local = [pltpu.make_async_copy(k_of(kv), k_out.at[me, rows], own_sem.at[0]),
             pltpu.make_async_copy(q_of(kv), q_out.at[rows], own_sem.at[1]),
             pltpu.make_async_copy(tag_ref, tag_out.at[me], own_sem.at[2])]
    for copy in k_sends + local:
        copy.start()
    pieces = []
    for i in range(groups):
        g = lax.rem(kv + groups - i, groups)
        pieces.append((g, pl.ds(pl.multiple_of(g * part, part), part)))

    def along_z(b, piece):
        g, at = piece
        return hop(k_out.at[b, at], k_out.at[b, at], z_send.at[b, g], k_recv.at[b, g], {"seq": me + 2})

    def across_x(b, piece):
        g, at = piece
        return hop(k_out.at[b, at], k_out.at[b, at], x_send.at[b, g], k_recv.at[b, g],
                   {"seq": me + 1 - 2 * x})

    for d in range(z_count):
        b = me - 2 * d
        if d == 1:
            for copy in q_sends + tag_sends:
                copy.start()
        for i, piece in enumerate(pieces):
            if d == 0:
                if i == 0:
                    local[0].wait()
                else:
                    g, at = piece
                    hop(k_out.at[me, at], k_out.at[me, at], kg_send.at[i], kg_recv.at[i],
                        {"kvh": g}).wait_recv()

            @pl.when(z >= d)
            def _():
                if d > 0:
                    along_z(b, piece).wait_recv()

                @pl.when(z < z_count - 1)
                def _():
                    along_z(b, piece).start()

                @pl.when((x == 0) | (d > 0))
                def _():
                    across_x(b, piece).start()

    for d in range(z_count):
        b = me - 2 * d
        other = b + 1 - 2 * x
        for piece in pieces:
            @pl.when((z >= d) & ((x == 1) | (d > 0)))
            def _():
                across_x(other, piece).wait_recv()

            @pl.when((z >= d) & (z < z_count - 1))
            def _():
                along_z(b, piece).wait_send()

            @pl.when((z >= d) & ((x == 0) | (d > 0)))
            def _():
                across_x(b, piece).wait_send()

    for copy in k_sends:
        copy.wait_send()
    for copy in local[1:]:
        copy.wait()
    for copy in q_sends + tag_sends:
        copy.wait()


def gathered(queries, keys, tags):
    peers, groups = lax.axis_size("seq"), lax.axis_size("kvh")
    part = queries.shape[0]
    anywhere = pl.BlockSpec(memory_space=pl.ANY)
    dma = pltpu.SemaphoreType.DMA
    return pl.pallas_call(
        functools.partial(gather_kernel, peers, groups),
        out_shape=(
            jax.ShapeDtypeStruct((part * groups, queries.shape[1] // groups), queries.dtype),
            jax.ShapeDtypeStruct((peers, part * groups, keys.shape[1] // groups), keys.dtype),
            jax.ShapeDtypeStruct((peers, 1, tags.shape[1]), tags.dtype),
        ),
        in_specs=[anywhere] * 3,
        out_specs=(pl.BlockSpec(memory_space=pltpu.VMEM),) * 3,
        scratch_shapes=[dma((3,)), dma((groups,)), dma((groups,)), dma((groups,)), dma((groups,)),
                        dma((peers,)), dma((peers,))] + [dma((peers, groups))] * 3,
        compiler_params=pltpu.CompilerParams(collective_id=0, has_side_effects=True,
                                             vmem_limit_bytes=4 * 1024 * 1024),
    )(queries, keys, tags)


def return_kernel(peers, part_ref, out_ref, got, send_sem, recv_sem):
    me = lax.axis_index("seq")
    meet(peers, 1)

    def send(to):
        return hop(part_ref.at[to], got.at[me], send_sem.at[to], recv_sem.at[me], {"seq": to})

    def arrival(i):
        return hop(part_ref.at[i], got.at[i], send_sem.at[i], recv_sem.at[i], {"seq": i})

    for j in range(peers):
        @pl.when(j < me)
        def _():
            send(j).start()
    out_ref[...] = part_ref[me]
    for i in range(peers):
        @pl.when(i > me)
        def _():
            arrival(i).wait_recv()
            out_ref[...] += got[i]
    for j in range(peers):
        @pl.when(j < me)
        def _():
            send(j).wait_send()


def returned(partials):
    peers = lax.axis_size("seq")
    vmem = pl.BlockSpec(memory_space=pltpu.VMEM)
    dma = pltpu.SemaphoreType.DMA
    return pl.pallas_call(
        functools.partial(return_kernel, peers),
        out_shape=jax.ShapeDtypeStruct(partials.shape[1:], partials.dtype),
        in_specs=[vmem],
        out_specs=vmem,
        scratch_shapes=[pltpu.VMEM(partials.shape, partials.dtype), dma((peers,)), dma((peers,))],
        compiler_params=pltpu.CompilerParams(collective_id=1, has_side_effects=True,
                                             vmem_limit_bytes=4 * 1024 * 1024),
    )(partials)


def reach_body(queries, keys, doc_ids):
    tags = (doc_ids + 1).reshape(1, -1)
    shard_len = tags.shape[1]
    q, k, all_tags = gathered(queries, keys, tags)
    own = lax.axis_index("seq").reshape(1)
    partials = window_columns(own, q, k.reshape(-1, k.shape[2]), tags.reshape(shard_len, 1), all_tags)
    return returned(partials)


def body(queries, keys, doc_ids):
    q = lax.all_to_all(queries, "kvh", split_axis=1, concat_axis=0, tiled=True)
    k = lax.all_to_all(keys, "kvh", split_axis=1, concat_axis=0, tiled=True)
    peers = lax.axis_size("seq")
    me = lax.axis_index("seq")
    shard_len = q.shape[0]
    slots = min(REACH_DEV, peers)
    start = jnp.maximum(me - (slots - 1), 0)
    own = me - start
    tags = doc_ids + 1
    all_keys = lax.all_gather(k, "seq", axis=0, tiled=True)
    all_tags = lax.all_gather(tags, "seq", axis=0, tiled=False)
    if peers > slots:
        all_keys = lax.dynamic_slice_in_dim(all_keys, start * shard_len, slots * shard_len, 0)
        all_tags = lax.dynamic_slice_in_dim(all_tags, start, slots, 0)
    partials = window_columns(own.reshape(1), q, all_keys, tags.reshape(shard_len, 1),
                              all_tags.reshape(slots, 1, shard_len))
    if peers > slots:
        spread = jnp.zeros((peers,) + partials.shape[1:], jnp.float32)
        partials = lax.dynamic_update_slice_in_dim(spread, partials, start, 0)
    back = lax.all_to_all(partials, "seq", split_axis=0, concat_axis=0, tiled=True)
    return jnp.sum(back, axis=0)


def solution(mesh):
    in_specs = (P(("seq", "kvh"), None), P(("seq", "kvh"), None), P("seq"))
    out_specs = P("kvh", "seq")
    whole_reach = mesh.shape["seq"] == REACH_DEV
    part = reach_body if whole_reach else body
    return jax.shard_map(part, mesh=mesh, in_specs=in_specs, out_specs=out_specs, check_vma=False)
```

```python
import functools
import math

import jax
import jax.numpy as jnp
from jax import lax
from jax.experimental import pallas as pl
from jax.experimental.pallas import tpu as pltpu
from jax.sharding import PartitionSpec as P

HD = 128
QPG = 5
REACH_DEV = 8
TILE = 512
STEP = 32
MASKED_SCORE = -1e30
ALLOWED_CAP = 3e38
EXP2_SCALE = math.log2(math.e) / math.sqrt(HD)


def score_kernel(own_ref, q_ref, k_ref, qtag_ref, ktag_ref, out_ref,
                 s0_ref, s1_ref, s2_ref, cap_ref, top_ref, max_ref, total_ref, inv_ref):
    rows = q_ref.shape[0]
    heads = q_ref.shape[1] // HD
    slots, _, block = ktag_ref.shape
    s_refs = (s0_ref, s1_ref, s2_ref)
    tile = s0_ref.shape[1]
    tiles = rows // tile
    units = heads * tiles
    own = own_ref[0]
    first_tag = jnp.min(qtag_ref[...])
    slot_of = lax.broadcasted_iota(jnp.int32, ktag_ref.shape, 0)
    ahead = jnp.sum(jnp.where((ktag_ref[...] < first_tag) & (slot_of < own), 1.0, 0.0))
    lo = ahead.astype(jnp.int32) // block
    hi = own + 1
    out_ref[...] = jnp.zeros_like(out_ref)

    row_pos = own * block + lax.broadcasted_iota(jnp.int32, (rows, block), 0)
    col_off = lax.broadcasted_iota(jnp.int32, (rows, block), 1)

    @pl.loop(lo, hi)
    def _(c):
        allowed = (ktag_ref[c] == qtag_ref[...]) & (col_off + c * block <= row_pos)
        cap_ref[c] = jnp.where(allowed, ALLOWED_CAP, MASKED_SCORE)

    def lane_tiles(x):
        return [x[:, i * HD:(i + 1) * HD] for i in range(block // HD)]

    def score_step(u, c):
        h, t = u // tiles, u % tiles
        first = t * tile
        q = q_ref[first:first + tile, h * HD:(h + 1) * HD]
        k = k_ref[pl.ds(pl.multiple_of(c * block, block), block),
                  h // QPG * HD:(h // QPG + 1) * HD]
        s_ref = s_refs[u % 3]
        s = lax.dot_general(q, k, (((1,), (1,)), ((), ())), preferred_element_type=jnp.float32)
        for r in range(0, tile, STEP):
            here = jnp.minimum(s[r:r + STEP], cap_ref[c, first + r:first + r + STEP, :])
            s_ref[c, r:r + STEP] = here
            top_ref[r:r + STEP] = functools.reduce(jnp.maximum, lane_tiles(here), top_ref[r:r + STEP])

    def exp_step(u, c):
        s_ref = s_refs[u % 3]
        for r in range(0, tile, STEP):
            row_max = max_ref[r:r + STEP]
            total = total_ref[r:r + STEP]
            for i in range(block // HD):
                cols = slice(i * HD, (i + 1) * HD)
                e = jnp.exp2((s_ref[c, r:r + STEP, cols] - row_max) * EXP2_SCALE)
                s_ref[c, r:r + STEP, cols] = e
                total = total + e
            total_ref[r:r + STEP] = total

    def column_step(u, c):
        s_ref = s_refs[u % 3]
        sums = [jnp.zeros((8, HD), jnp.float32)] * (block // HD)
        for r in range(0, tile, 8):
            inv = inv_ref[r:r + 8]
            sums = [acc + s_ref[c, r:r + 8, i * HD:(i + 1) * HD] * inv
                    for i, acc in enumerate(sums)]
        out_ref[c, u // tiles:u // tiles + 1, :] += jnp.sum(jnp.concatenate(sums, axis=1), axis=0, keepdims=True)

    def turn(u, stages):
        if 0 in stages:
            top_ref[...] = jnp.full(top_ref.shape, MASKED_SCORE, jnp.float32)
        if 1 in stages:
            total_ref[...] = jnp.zeros(total_ref.shape, jnp.float32)

        def steps(chunks):
            for c in chunks:
                if 0 in stages:
                    score_step(u, c)
            for c in chunks:
                if 1 in stages:
                    exp_step(u - 1, c)
            for c in chunks:
                if 2 in stages:
                    column_step(u - 2, c)

        @pl.loop(0, (hi - lo) // 2)
        def _(p):
            steps((lo + 2 * p, lo + 2 * p + 1))

        @pl.when((hi - lo) % 2 == 1)
        def _():
            steps((hi - 1,))

        if 0 in stages:
            row_max = jnp.max(top_ref[...], axis=-1, keepdims=True)
            max_ref[...] = jnp.broadcast_to(row_max, max_ref.shape)
        if 1 in stages:
            inv = 1.0 / jnp.sum(total_ref[...], axis=-1, keepdims=True)
            inv_ref[...] = jnp.broadcast_to(inv, inv_ref.shape)

    for u in range(units + 2):
        turn(u, [i for i in range(3) if 0 <= u - i < units])


def window_columns(own, q, k, qtag, ktag):
    rows = q.shape[0]
    heads = q.shape[1] // HD
    slots, _, block = ktag.shape
    vmem = pl.BlockSpec(memory_space=pltpu.VMEM)
    return pl.pallas_call(
        score_kernel,
        out_shape=jax.ShapeDtypeStruct((slots, heads, block), jnp.float32),
        in_specs=[pl.BlockSpec(memory_space=pltpu.SMEM), vmem, vmem, vmem, vmem],
        out_specs=vmem,
        scratch_shapes=[pltpu.VMEM((slots, TILE, block), jnp.float32)] * 3 + [
            pltpu.VMEM((slots, rows, block), jnp.float32),
        ] + [pltpu.VMEM((TILE, HD), jnp.float32)] * 4,
        compiler_params=pltpu.CompilerParams(vmem_limit_bytes=40 * 1024 * 1024),
    )(own, q, k, qtag, ktag)


def hop(src, dst, send_sem, recv_sem, device_id):
    return pltpu.make_async_remote_copy(
        src_ref=src, dst_ref=dst, send_sem=send_sem, recv_sem=recv_sem,
        device_id=device_id, device_id_type=pl.DeviceIdType.MESH)


def meet(seq_peers, kvh_peers):
    barrier = pltpu.get_barrier_semaphore()
    me, kv = lax.axis_index("seq"), lax.axis_index("kvh")
    for i in range(1, seq_peers):
        pl.semaphore_signal(barrier, inc=1, device_id={"seq": lax.rem(me + i, seq_peers)},
                            device_id_type=pl.DeviceIdType.MESH)
    for i in range(1, kvh_peers):
        pl.semaphore_signal(barrier, inc=1, device_id={"kvh": lax.rem(kv + i, kvh_peers)},
                            device_id_type=pl.DeviceIdType.MESH)
    pl.semaphore_wait(barrier, seq_peers + kvh_peers - 2)


def gather_kernel(peers, groups, q_ref, k_ref, tag_ref, q_out, k_out, tag_out,
                  own_sem, kg_send, kg_recv, qg_send, qg_recv, tag_send, tag_recv,
                  z_send, x_send, k_recv):
    me, kv = lax.axis_index("seq"), lax.axis_index("kvh")
    z, x = me // 2, lax.rem(me, 2)
    z_count = peers // 2
    part = q_ref.shape[0]
    q_cols, k_cols = q_out.shape[1], k_out.shape[2]
    meet(peers, groups)

    rows = pl.ds(pl.multiple_of(kv * part, part), part)

    def q_of(g):
        return q_ref.at[:, pl.ds(pl.multiple_of(g * q_cols, q_cols), q_cols)]

    def k_of(g):
        return k_ref.at[:, pl.ds(pl.multiple_of(g * k_cols, k_cols), k_cols)]

    k_sends, q_sends, tag_sends = [], [], []
    for i in range(1, groups):
        to = lax.rem(kv + i, groups)
        k_sends.append(hop(k_of(to), k_out.at[me, rows], kg_send.at[i], kg_recv.at[i], {"kvh": to}))
        q_sends.append(hop(q_of(to), q_out.at[rows], qg_send.at[i], qg_recv.at[i], {"kvh": to}))
    for i in range(1, peers):
        to = lax.rem(me + i, peers)
        tag_sends.append(hop(tag_ref, tag_out.at[me], tag_send.at[i], tag_recv.at[i], {"seq": to}))
    local = [pltpu.make_async_copy(k_of(kv), k_out.at[me, rows], own_sem.at[0]),
             pltpu.make_async_copy(q_of(kv), q_out.at[rows], own_sem.at[1]),
             pltpu.make_async_copy(tag_ref, tag_out.at[me], own_sem.at[2])]
    for copy in k_sends + local:
        copy.start()
    pieces = []
    for i in range(groups):
        g = lax.rem(kv + groups - i, groups)
        pieces.append((g, pl.ds(pl.multiple_of(g * part, part), part)))

    def along_z(b, piece):
        g, at = piece
        return hop(k_out.at[b, at], k_out.at[b, at], z_send.at[b, g], k_recv.at[b, g], {"seq": me + 2})

    def across_x(b, piece):
        g, at = piece
        return hop(k_out.at[b, at], k_out.at[b, at], x_send.at[b, g], k_recv.at[b, g],
                   {"seq": me + 1 - 2 * x})

    for d in range(z_count):
        b = me - 2 * d
        if d == 1:
            for copy in q_sends + tag_sends:
                copy.start()
        for i, piece in enumerate(pieces):
            if d == 0:
                if i == 0:
                    local[0].wait()
                else:
                    g, at = piece
                    hop(k_out.at[me, at], k_out.at[me, at], kg_send.at[i], kg_recv.at[i],
                        {"kvh": g}).wait_recv()

            @pl.when(z >= d)
            def _():
                if d > 0:
                    along_z(b, piece).wait_recv()

                @pl.when(z < z_count - 1)
                def _():
                    along_z(b, piece).start()

                @pl.when((x == 0) | (d > 0))
                def _():
                    across_x(b, piece).start()

    for d in range(z_count):
        b = me - 2 * d
        other = b + 1 - 2 * x
        for piece in pieces:
            @pl.when((z >= d) & ((x == 1) | (d > 0)))
            def _():
                across_x(other, piece).wait_recv()

            @pl.when((z >= d) & (z < z_count - 1))
            def _():
                along_z(b, piece).wait_send()

            @pl.when((z >= d) & ((x == 0) | (d > 0)))
            def _():
                across_x(b, piece).wait_send()

    for copy in k_sends:
        copy.wait_send()
    for copy in local[1:]:
        copy.wait()
    for copy in q_sends + tag_sends:
        copy.wait()


def gathered(queries, keys, tags):
    peers, groups = lax.axis_size("seq"), lax.axis_size("kvh")
    part = queries.shape[0]
    anywhere = pl.BlockSpec(memory_space=pl.ANY)
    dma = pltpu.SemaphoreType.DMA
    return pl.pallas_call(
        functools.partial(gather_kernel, peers, groups),
        out_shape=(
            jax.ShapeDtypeStruct((part * groups, queries.shape[1] // groups), queries.dtype),
            jax.ShapeDtypeStruct((peers, part * groups, keys.shape[1] // groups), keys.dtype),
            jax.ShapeDtypeStruct((peers, 1, tags.shape[1]), tags.dtype),
        ),
        in_specs=[anywhere] * 3,
        out_specs=(pl.BlockSpec(memory_space=pltpu.VMEM),) * 3,
        scratch_shapes=[dma((3,)), dma((groups,)), dma((groups,)), dma((groups,)), dma((groups,)),
                        dma((peers,)), dma((peers,))] + [dma((peers, groups))] * 3,
        compiler_params=pltpu.CompilerParams(collective_id=0, has_side_effects=True,
                                             vmem_limit_bytes=4 * 1024 * 1024),
    )(queries, keys, tags)


def return_kernel(peers, part_ref, out_ref, got, send_sem, recv_sem):
    me = lax.axis_index("seq")
    meet(peers, 1)

    def send(to):
        return hop(part_ref.at[to], got.at[me], send_sem.at[to], recv_sem.at[me], {"seq": to})

    def arrival(i):
        return hop(part_ref.at[i], got.at[i], send_sem.at[i], recv_sem.at[i], {"seq": i})

    for j in range(peers):
        @pl.when(j < me)
        def _():
            send(j).start()
    out_ref[...] = part_ref[me]
    for i in range(peers):
        @pl.when(i > me)
        def _():
            arrival(i).wait_recv()
            out_ref[...] += got[i]
    for j in range(peers):
        @pl.when(j < me)
        def _():
            send(j).wait_send()


def returned(partials):
    peers = lax.axis_size("seq")
    vmem = pl.BlockSpec(memory_space=pltpu.VMEM)
    dma = pltpu.SemaphoreType.DMA
    return pl.pallas_call(
        functools.partial(return_kernel, peers),
        out_shape=jax.ShapeDtypeStruct(partials.shape[1:], partials.dtype),
        in_specs=[vmem],
        out_specs=vmem,
        scratch_shapes=[pltpu.VMEM(partials.shape, partials.dtype), dma((peers,)), dma((peers,))],
        compiler_params=pltpu.CompilerParams(collective_id=1, has_side_effects=True,
                                             vmem_limit_bytes=4 * 1024 * 1024),
    )(partials)


def reach_body(queries, keys, doc_ids):
    tags = (doc_ids + 1).reshape(1, -1)
    shard_len = tags.shape[1]
    q, k, all_tags = gathered(queries, keys, tags)
    own = lax.axis_index("seq").reshape(1)
    partials = window_columns(own, q, k.reshape(-1, k.shape[2]), tags.reshape(shard_len, 1), all_tags)
    return returned(partials)


def body(queries, keys, doc_ids):
    q = lax.all_to_all(queries, "kvh", split_axis=1, concat_axis=0, tiled=True)
    k = lax.all_to_all(keys, "kvh", split_axis=1, concat_axis=0, tiled=True)
    peers = lax.axis_size("seq")
    me = lax.axis_index("seq")
    shard_len = q.shape[0]
    slots = min(REACH_DEV, peers)
    start = jnp.maximum(me - (slots - 1), 0)
    own = me - start
    tags = doc_ids + 1
    all_keys = lax.all_gather(k, "seq", axis=0, tiled=True)
    all_tags = lax.all_gather(tags, "seq", axis=0, tiled=False)
    if peers > slots:
        all_keys = lax.dynamic_slice_in_dim(all_keys, start * shard_len, slots * shard_len, 0)
        all_tags = lax.dynamic_slice_in_dim(all_tags, start, slots, 0)
    partials = window_columns(own.reshape(1), q, all_keys, tags.reshape(shard_len, 1),
                              all_tags.reshape(slots, 1, shard_len))
    if peers > slots:
        spread = jnp.zeros((peers,) + partials.shape[1:], jnp.float32)
        partials = lax.dynamic_update_slice_in_dim(spread, partials, start, 0)
    back = lax.all_to_all(partials, "seq", split_axis=0, concat_axis=0, tiled=True)
    return jnp.sum(back, axis=0)


def solution(mesh):
    in_specs = (P(("seq", "kvh"), None), P(("seq", "kvh"), None), P("seq"))
    out_specs = P("kvh", "seq")
    whole_reach = mesh.shape["seq"] == REACH_DEV
    part = reach_body if whole_reach else body
    return jax.shard_map(part, mesh=mesh, in_specs=in_specs, out_specs=out_specs, check_vma=False)
```
